32 devices in a mesh: ctx: 4 (over x, core), tp: 4 (over z), dp: 2 (over y).
Axes of the slice: x: 2, y: 2, z: 4, core: 2. Of those that a mesh axis runs over, the one named last changes fastest.
Arguments:
- activations: bfloat16 [4096, 4096], P(('ctx', 'tp', 'dp')), may hold values from -6 to 6
- out_grad: bfloat16 [4096, 4096], P(('ctx', 'tp', 'dp')), may hold values from -6 to 6
- routes: int32 [4096, 8], P(('ctx', 'tp', 'dp')), may hold values from 0 to 31, all different within a row; in each aligned block of 128 rows (0 to 127, 128 to 255, ...) at most 48 rows name the same one
- gate_probs: bfloat16 [4096, 8], P(('ctx', 'tp', 'dp')), may hold values from 0.049804688 to 0.59765625
- saved_pre: bfloat16 [16, 2, 768, 1536], P(('ctx', 'tp'), 'dp'), may hold values from -6 to 6
- expert_weights: bfloat16 [16, 4096, 2304], P(('ctx', 'tp'), 'dp'), may hold values from -0.09375 to 0.09375
Outputs:
- input_grad: bfloat16 [4096, 4096], P(('ctx', 'tp', 'dp'))
- prob_grad: bfloat16 [4096, 8], P(('ctx', 'tp', 'dp'))
- weight_grad: bfloat16 [16, 4096, 2304], P(('ctx', 'tp'), 'dp')
The draws below stay inside these ranges and needn't reach their ends.
Inputs may be any that keep to these rules, and one draw needn't show every extreme that they name: `routes`: each row names 8 different experts. Within the rows of one device (aligned blocks of 128 rows) no expert is named more than 48 times, a bound that some block reaches.
All inputs are finite; a program needn't handle non-finite values.
Results may differ from the reference program's by a relative error of at most 0.02.
Values may be sent and summed in bfloat16 or wider, within the bound.
A program may use at most 192 MiB of HBM per device.

```python
import math
import jax
import jax.numpy as jnp
import numpy as np
from jax import lax

D = 4096
H = 768
TOP = 8
T_DEV = 128
EXPERTS = 16
ROUTED = 32
CAP = 48
SLOTS = 768
TOKENS = 4096
N_DP = 2


def block_scale(own_key, extent, shards, smallest, high):
    loudness = 1.0
    for axis_at, shards_of in shards:
        draws = jax.random.uniform(jax.random.fold_in(jax.random.fold_in(own_key, 6), axis_at), (shards_of,), jnp.float32, smallest / len(shards), high / len(shards))
        loudness = loudness * jnp.repeat(jnp.exp(draws), extent[axis_at] // shards_of).reshape((-1,) + (1,) * (len(extent) - 1 - axis_at))
    return loudness


def assign_block(rng, own, number, rows, count, top, most, slope):
    ranking = jax.random.permutation(rng, count)
    heavy_load, usual = portions_of(count, rows * top, most, slope, True), portions_of(count, rows * top, most, slope, False)
    places = jnp.arange(count)

    def named(sizes, offset_by):
        used = int((sizes > 0).sum())
        fixed = max(1, used // 4)
        moved = fixed + (places - fixed + offset_by * (used - fixed)) % max(1, count - fixed)
        return jnp.zeros((count,), jnp.int32).at[ranking[jnp.where(places < fixed, places, moved)]].set(jnp.asarray(sizes, jnp.int32))

    sizes = jnp.where(number % 4 == 0, named(heavy_load, number // 4), named(usual, number - number // 4 - 1))
    mixed = jax.random.permutation(jax.random.fold_in(own, 3), count)
    giver, receiver = mixed[0:count // 2 * 2:2], mixed[1:count // 2 * 2:2]
    room = jnp.minimum(sizes[giver] - 1, most - sizes[receiver]) // 2
    room = jnp.where((giver == ranking[0]) | (receiver == ranking[0]) | (sizes[receiver] == 0), 0, jnp.maximum(room, 0))
    moved = jax.random.randint(jax.random.fold_in(own, 4), (count // 2,), 0, 1 << 20) % (room + 1)
    sizes = sizes.at[giver].add(-moved).at[receiver].add(moved)
    labels = jnp.searchsorted(jnp.cumsum(sizes), jnp.arange(rows * top), side="right").astype(jnp.int32)
    listing = labels.reshape(top, rows).T
    listing = listing[jax.random.permutation(jax.random.fold_in(own, 1), rows)]
    offset_by = jax.random.randint(jax.random.fold_in(own, 2), (rows, 1), 0, top)
    return jnp.take_along_axis(listing, (jnp.arange(top)[None, :] + offset_by) % top, axis=1)


def portions_of(number_of, total, bound, slope, full):
    loads = [(1 << 20) // math.isqrt(rank ** slope) + 1 for rank in range(1, number_of + 1)]
    largest = bound if full else min(bound, max(-(-total // number_of), total * loads[0] // sum(loads)))
    least = 1 if total - largest >= number_of - 1 else 0
    counts, spare = [largest] + [least] * (number_of - 1), total - largest - least * (number_of - 1)
    while spare > 0:
        movable = [i for i in range(1, number_of) if counts[i] < largest] or [i for i in range(1, number_of) if counts[i] < bound]
        mass, left = sum([loads[i] for i in movable]), spare
        for i in movable:
            extra = min(bound - counts[i], max(1, left * loads[i] // mass), spare)
            counts[i] = counts[i] + extra
            spare = spare - extra
    return np.array(counts)


def normal_values(key, extent, spread, bound, split=(), held_as=jnp.bfloat16):
    factor_of = block_scale(key, extent, split, -0.22, 0.18) if split else 1.0
    drawn = jax.random.normal(key, extent, jnp.float32) * spread * factor_of
    return jnp.minimum(jnp.maximum(drawn, -bound), bound).astype(held_as)


def setup_inputs(seed: int = 0) -> dict:
    streams_of = jax.random.split(jax.random.key(seed), 7)
    activations = normal_values(streams_of[0], (TOKENS, D), 1.0, 6.0, ((0, 32),))
    out_grad = normal_values(streams_of[1], (TOKENS, D), 1.0, 6.0, ((0, 32),))
    routes_keys = jax.random.split(jax.random.fold_in(streams_of[2], 1), TOKENS // T_DEV)
    routes_turns = jax.random.permutation(jax.random.fold_in(streams_of[2], 3), TOKENS // T_DEV)
    routes = jax.vmap(lambda own, number: assign_block(jax.random.fold_in(streams_of[2], 2), own, number, T_DEV, ROUTED, TOP, CAP, 1))(routes_keys, routes_turns).reshape((TOKENS, TOP))
    gate_probs = jnp.clip(0.049804688 + 0.54785156 * jax.random.uniform(streams_of[3], (TOKENS, TOP), jnp.float32) ** block_scale(streams_of[3], (TOKENS, TOP), ((0, 32),), -0.2, 0.2), 0.049804688, 0.59765625).astype(jnp.bfloat16)
    saved_pre = normal_values(streams_of[4], (EXPERTS, N_DP, SLOTS, 2 * H), 1.0, 6.0, ((0, 16), (1, 2)))
    expert_weights = normal_values(streams_of[5], (EXPERTS, D, 3 * H), D ** -0.5, 0.09375, ((0, 16), (1, 2)))
    return dict(activations=activations, out_grad=out_grad, routes=routes, gate_probs=gate_probs, saved_pre=saved_pre, expert_weights=expert_weights)


def slot_table(routes):
    blocks = TOKENS // T_DEV
    per_block = routes.reshape(blocks, T_DEV * TOP).astype(jnp.int32)
    in_window = per_block < EXPERTS
    onehot = (per_block[:, :, None] == jnp.arange(EXPERTS, dtype=jnp.int32)[None, None, :]).astype(jnp.int32)
    position = jnp.sum(jnp.cumsum(onehot, axis=1) * onehot, axis=2) - 1
    block_ids = jnp.arange(blocks, dtype=jnp.int32)[:, None]
    source = block_ids // N_DP
    replica = block_ids % N_DP
    slot_total = EXPERTS * N_DP * SLOTS
    flat_slot = (per_block * N_DP + replica) * SLOTS + source * CAP + position
    flat_slot = jnp.where(in_window, flat_slot, slot_total).astype(jnp.int32)
    route_ids = jnp.arange(TOKENS * TOP, dtype=jnp.int32)
    slot_routes = jnp.full((slot_total,), TOKENS * TOP, jnp.int32)
    slot_routes = slot_routes.at[flat_slot.reshape(-1)].set(route_ids, mode="drop")
    return slot_routes.reshape(EXPERTS, N_DP, SLOTS)


def expert_math(expert_rows, expert_grads, expert_probs, saved_rows, weights):
    pre_gate = saved_rows[:, :H].astype(jnp.float32)
    pre_up = saved_rows[:, H:].astype(jnp.float32)
    sigmoid_gate = jax.nn.sigmoid(pre_gate)
    activated = pre_gate * sigmoid_gate
    hidden_act = activated * pre_up
    down_grad = jnp.dot(expert_grads, weights[:, 2 * H:], preferred_element_type=jnp.float32)
    slot_prob = jnp.sum(hidden_act * down_grad, axis=1).astype(jnp.bfloat16)
    prob_column = expert_probs[:, None]
    scaled_grad = prob_column * down_grad
    gate_up_grad = jnp.concatenate(
        [scaled_grad * pre_up * sigmoid_gate * (1.0 + pre_gate * (1.0 - sigmoid_gate)), scaled_grad * activated],
        axis=1).astype(jnp.bfloat16)
    scaled_hidden = (prob_column * hidden_act).astype(jnp.bfloat16)
    row_grad = lax.dot_general(gate_up_grad, weights[:, :2 * H], (((1,), (1,)), ((), ())),
                               preferred_element_type=jnp.float32).astype(jnp.bfloat16)
    gate_up_term = lax.dot_general(expert_rows, gate_up_grad, (((0,), (0,)), ((), ())),
                                   preferred_element_type=jnp.float32)
    down_term = lax.dot_general(expert_grads, scaled_hidden, (((0,), (0,)), ((), ())),
                                preferred_element_type=jnp.float32)
    return slot_prob, row_grad, jnp.concatenate([gate_up_term, down_term], axis=1)


def reference(activations, out_grad, routes, gate_probs, saved_pre, expert_weights):
    slot_routes = slot_table(routes)
    route_total = TOKENS * TOP
    flat_probs = gate_probs.reshape(-1)

    def one_expert(accum, inputs):
        input_acc, prob_acc = accum
        expert_routes, saved_block, weights = inputs
        partial_value = jnp.zeros((D, 3 * H), jnp.float32)
        for replica in range(N_DP):
            routes_here = expert_routes[replica].astype(jnp.int32)
            filled = routes_here < route_total
            safe_ids = jnp.minimum(routes_here, route_total - 1).astype(jnp.int32)
            token_ids = (safe_ids // TOP).astype(jnp.int32)
            expert_rows = jnp.where(filled[:, None], activations[token_ids], jnp.zeros((), jnp.bfloat16))
            expert_grads = jnp.where(filled[:, None], out_grad[token_ids], jnp.zeros((), jnp.bfloat16))
            expert_probs = jnp.where(filled, flat_probs[safe_ids], jnp.zeros((), jnp.bfloat16)).astype(jnp.float32)
            slot_prob, row_grad, contrib = expert_math(expert_rows, expert_grads, expert_probs,
                                                       saved_block[replica], weights)
            rounded = lax.optimization_barrier(contrib.astype(jnp.bfloat16))
            partial_value = partial_value + rounded.astype(jnp.float32)
            target_tokens = jnp.where(filled, token_ids, TOKENS).astype(jnp.int32)
            input_acc = input_acc.at[target_tokens].add(row_grad.astype(jnp.float32), mode="drop")
            target_routes = jnp.where(filled, safe_ids, route_total).astype(jnp.int32)
            prob_acc = prob_acc.at[target_routes].set(slot_prob.astype(jnp.float32), mode="drop")
        return (input_acc, prob_acc), partial_value.astype(jnp.bfloat16)

    start = (jnp.zeros((TOKENS, D), jnp.float32), jnp.zeros((route_total,), jnp.float32))
    (input_acc, prob_acc), weight_grad = lax.scan(one_expert, start, (slot_routes, saved_pre, expert_weights))
    input_grad = input_acc.astype(jnp.bfloat16)
    prob_grad = prob_acc.reshape(TOKENS, TOP).astype(jnp.bfloat16)
    return (input_grad, prob_grad, weight_grad)
```

```python
import jax
import jax.numpy as jnp
from jax import lax
from jax.sharding import PartitionSpec as P

PLANE = ("ctx", "tp")
F32 = jnp.float32
BF16 = jnp.bfloat16


def gather_plane(x):
    return lax.all_gather(x, PLANE, axis=0, tiled=False)


def scatter_plane(x):
    return lax.psum_scatter(x, PLANE, scatter_dimension=0, tiled=False)


def body(activations, out_grad, routes, gate_probs, saved_pre, expert_weights):
    tokens, width = activations.shape
    top_k = routes.shape[1]
    sources = lax.axis_size("ctx") * lax.axis_size("tp")
    expert = lax.axis_index(PLANE)
    replica = lax.axis_index("dp")
    slots = saved_pre.shape[2]
    cap = slots // sources
    hidden = saved_pre.shape[3] // 2
    half = width // 2
    swap = [(0, 1), (1, 0)]

    def halves(x):
        low, high = x[:, :half], x[:, half:]
        keep = jnp.where(replica == 0, low, high)
        give = jnp.where(replica == 0, high, low)
        return keep, give

    grad_keep, grad_give = halves(out_grad)
    act_keep, act_give = halves(activations)
    grad_other = lax.ppermute(grad_give, "dp", swap)
    act_other = lax.ppermute(act_give, "dp", swap)
    own_pre = saved_pre[0, 0]
    other_pre = lax.ppermute(own_pre, "dp", swap)

    routes_own = lax.all_gather(routes, PLANE, axis=0, tiled=False)
    probs_own = lax.all_gather(gate_probs, PLANE, axis=0, tiled=False)
    routes_other = lax.ppermute(routes_own, "dp", swap)
    probs_other = lax.ppermute(probs_own, "dp", swap)

    earlier = (
        lax.broadcasted_iota(jnp.int32, (tokens, tokens), 0)
        < lax.broadcasted_iota(jnp.int32, (tokens, tokens), 1)
    ).astype(BF16)

    def select(routes_in, probs_in):
        hit = routes_in == expert
        named = jnp.any(hit, axis=2)
        prob = jnp.sum(jnp.where(hit, probs_in.astype(F32), 0.0), axis=2)
        rank = jnp.dot(named.astype(BF16), earlier, preferred_element_type=F32)
        place = lax.broadcasted_iota(jnp.int32, (sources, cap, tokens), 1)
        chosen = named[:, None, :] & (rank.astype(jnp.int32)[:, None, :] == place)
        prob_column = jnp.sum(jnp.where(chosen, prob[:, None, :], 0.0), axis=2)
        return chosen.astype(BF16), prob_column.reshape(slots, 1)

    chosen = []
    columns = []
    for pair in ((routes_own, probs_own), (routes_other, probs_other)):
        c, p = select(*pair)
        chosen.append(c)
        columns.append(p)

    def pack(which, gathered):
        return jnp.einsum(
            "spt,std->spd", chosen[which], gathered, preferred_element_type=F32
        ).astype(BF16).reshape(slots, half)

    weights = expert_weights[0]
    down_part = weights[:, 2 * hidden :]
    gate_up_part = weights[:, : 2 * hidden]

    grad_rows = [pack(0, gather_plane(grad_keep)), pack(1, gather_plane(grad_other))]
    act_rows = [pack(0, gather_plane(act_keep)), pack(1, gather_plane(act_other))]
    part = [jnp.dot(g, down_part, preferred_element_type=F32) for g in grad_rows]
    arrived = [
        lax.ppermute(part[1].astype(BF16), "dp", swap),
        lax.ppermute(part[0].astype(BF16), "dp", swap),
    ]
    gate_up = []
    scaled = []
    token_probs = None
    for i, pre in enumerate((own_pre, other_pre)):
        down_grad = part[i] + arrived[i].astype(F32)
        gate = pre[:, :hidden].astype(F32)
        up = pre[:, hidden:].astype(F32)
        sig = jax.nn.sigmoid(gate)
        act = gate * sig
        hidden_act = act * up
        if i == 0:
            slot_prob = jnp.sum(hidden_act * down_grad, axis=1).astype(BF16)
            token_probs = jnp.sum(
                jnp.where(chosen[0] > 0, slot_prob.reshape(sources, cap, 1).astype(F32), 0.0),
                axis=1,
            ).astype(BF16)
        dh = columns[i] * down_grad
        gate_up.append(
            jnp.concatenate([dh * up * sig * (1.0 + gate * (1.0 - sig)), dh * act], axis=1).astype(
                BF16
            )
        )
        scaled.append((columns[i] * hidden_act).astype(BF16))

    summed = [None, None]
    for i in (1, 0):
        row_grad = lax.dot_general(
            gate_up[i], gate_up_part, (((1,), (1,)), ((), ())), preferred_element_type=F32
        ).astype(BF16)
        spread = jnp.einsum(
            "spt,spd->std",
            chosen[i],
            row_grad.reshape(sources, cap, half),
            preferred_element_type=F32,
        ).astype(BF16)
        summed[i] = scatter_plane(spread)

    def outer(rows, cols):
        return lax.dot_general(rows, cols, (((0,), (0,)), ((), ())), preferred_element_type=F32)

    gate_up_term = outer(act_rows[0], gate_up[0]) + outer(act_rows[1], gate_up[1])
    down_term = outer(grad_rows[0], scaled[0]) + outer(grad_rows[1], scaled[1])
    weight_grad = jnp.concatenate([gate_up_term.astype(BF16), down_term.astype(BF16)], axis=1)[None]

    far = lax.ppermute(summed[1], "dp", swap)
    near = summed[0]
    input_grad = jnp.concatenate(
        [jnp.where(replica == 0, near, far), jnp.where(replica == 0, far, near)], axis=1
    )
    back = lax.all_to_all(token_probs, PLANE, split_axis=0, concat_axis=0, tiled=True)
    experts = lax.broadcasted_iota(jnp.int32, (sources, tokens, top_k), 0)
    prob_grad = jnp.sum(
        jnp.where(routes[None] == experts, back[:, :, None].astype(F32), 0.0), axis=0
    ).astype(BF16)
    return (input_grad, prob_grad, weight_grad)


def solution(mesh):
    placed = (
        P(("ctx", "tp", "dp"), None),
        P(("ctx", "tp", "dp"), None),
        P(("ctx", "tp", "dp"), None),
        P(("ctx", "tp", "dp"), None),
        P(("ctx", "tp"), "dp", None, None),
        P(("ctx", "tp"), "dp", None),
    )
    return jax.shard_map(
        body,
        mesh=mesh,
        in_specs=placed,
        out_specs=(
            P(("ctx", "tp", "dp"), None),
            P(("ctx", "tp", "dp"), None),
            P(("ctx", "tp"), "dp", None),
        ),
        check_vma=False,
    )
```

```python
import jax
import jax.numpy as jnp
from jax import lax
from jax.experimental import pallas as pl
from jax.experimental.pallas import tpu as pltpu
from jax.sharding import PartitionSpec as P

PLANE = ("ctx", "tp")
F32 = jnp.float32
BF16 = jnp.bfloat16


def outer_kernel(a0, a1, g0, g1, u0, u1, s0, s1, out):
    def outer(rows, cols):
        return lax.dot_general(
            rows[...], cols[...], (((0,), (0,)), ((), ())), preferred_element_type=F32
        )

    wide = u0.shape[1]
    out[:, :wide] = (outer(a0, u0) + outer(a1, u1)).astype(BF16)
    out[:, wide:] = (outer(g0, s0) + outer(g1, s1)).astype(BF16)


def weight_outer(acts, grads, gate_up, scaled):
    slots, features = acts[0].shape
    wide, narrow = gate_up[0].shape[1], scaled[0].shape[1]
    tile = 256
    rows = pl.BlockSpec((slots, tile), lambda i: (0, i))
    whole = [pl.BlockSpec((slots, n), lambda i: (0, 0)) for n in (wide, wide, narrow, narrow)]
    return pl.pallas_call(
        outer_kernel,
        grid=(features // tile,),
        in_specs=[rows] * 4 + whole,
        out_specs=pl.BlockSpec((tile, wide + narrow), lambda i: (i, 0)),
        out_shape=jax.ShapeDtypeStruct((features, wide + narrow), BF16),
        compiler_params=pltpu.CompilerParams(vmem_limit_bytes=40 * 2**20),
        cost_estimate=pl.CostEstimate(
            flops=4 * slots * features * (wide + narrow),
            bytes_accessed=2 * (features * (4 * slots + wide + narrow) + 2 * slots * (wide + narrow)),
            transcendentals=0,
        ),
    )(*acts, *grads, *gate_up, *scaled)


def body(activations, out_grad, routes, gate_probs, saved_pre, expert_weights):
    tokens, width = activations.shape
    top_k = routes.shape[1]
    ctx_size = lax.axis_size("ctx")
    nz = lax.axis_size("tp")
    nx = ctx_size // 2
    sources = ctx_size * nz
    replica = lax.axis_index("dp")
    ctx_at = lax.axis_index("ctx")
    z_at = lax.axis_index("tp")
    x_at, core_at = ctx_at // 2, ctx_at % 2
    slots = saved_pre.shape[2]
    cap = slots // sources
    hidden = saved_pre.shape[3] // 2
    half = width // 2
    near = nx * nz

    def swap_dp(v):
        return lax.ppermute(v, "dp", [(0, 1), (1, 0)])

    def swap_core(v):
        return lax.ppermute(v, "ctx", [(i, i ^ 1) for i in range(ctx_size)])

    def move_x(v, by):
        pairs = [(i, (i // 2 + by) % nx * 2 + i % 2) for i in range(ctx_size)]
        return lax.ppermute(v, "ctx", pairs)

    def move_z(v, by):
        return lax.ppermute(v, "tp", [(i, (i + by) % nz) for i in range(nz)])

    def regroup(v):
        low, high = v[:, :half], v[:, half:]
        keep = jnp.where(replica == 0, low, high)
        other = swap_dp(jnp.where(replica == 0, high, low))
        return jnp.stack([keep, other])

    def gather_z(v):
        blocks = [v]
        for _ in range(1, nz):
            blocks.append(move_z(blocks[-1], 1))
        return blocks

    def permuted(rows_from, v):
        onehot = (rows_from[:, None] == jnp.arange(sources)[None, :]).astype(BF16)
        flat = v.reshape(sources, -1)
        moved = jnp.dot(onehot, flat, preferred_element_type=F32).astype(BF16)
        return moved.reshape(v.shape)

    note = jnp.concatenate([routes.astype(BF16), gate_probs], axis=1)
    column_notes = gather_z(jnp.stack([note, swap_dp(note)]))
    column_notes = jnp.stack(column_notes)
    spans = [column_notes] + [move_x(column_notes, t) for t in range(1, nx)]
    near_notes = jnp.stack(spans, axis=1).reshape(near, 2, tokens, 2 * top_k)
    notes = jnp.concatenate([near_notes, swap_core(near_notes)])

    order = jnp.arange(2 * near)
    src_core = jnp.bitwise_xor(order // near, core_at)
    src_z = (z_at - order // nx % nz) % nz
    src_x = (x_at - order % nx) % nx
    source_at = (src_x * 2 + src_core) * nz + src_z
    routes_at = notes[..., :top_k].astype(jnp.int32)
    probs_at = notes[..., top_k:].astype(F32)
    earlier = (
        lax.broadcasted_iota(jnp.int32, (tokens, tokens), 0)
        < lax.broadcasted_iota(jnp.int32, (tokens, tokens), 1)
    ).astype(BF16)

    def select(r, p, which):
        hit = r == which
        named = jnp.any(hit, axis=-1)
        prob = jnp.sum(jnp.where(hit, p, 0.0), axis=-1)
        rank = jnp.dot(named.astype(BF16), earlier, preferred_element_type=F32)
        place = lax.broadcasted_iota(jnp.int32, rank.shape[:2] + (cap, tokens), 2)
        chosen = named[:, :, None] & (rank.astype(jnp.int32)[:, :, None] == place)
        column = jnp.sum(jnp.where(chosen, prob[:, :, None], 0.0), axis=-1)
        return chosen, column

    mine = (x_at * 2 + core_at) * nz + z_at
    chosen_mine, column = select(routes_at, probs_at, mine)
    column_routes = column_notes[..., :top_k].astype(jnp.int32)
    column_probs = column_notes[..., top_k:].astype(F32)
    pick = []
    for t in range(nx):
        for cr in range(2):
            expert = ((x_at + t) % nx * 2 + jnp.bitwise_xor(core_at, cr)) * nz + z_at
            pick.append(select(column_routes, column_probs, expert)[0])
    pick = jnp.concatenate(pick, axis=2).astype(BF16)
    columns = column.reshape(2, slots, 1)

    from_slot = jnp.repeat(source_at, cap) * cap + jnp.tile(jnp.arange(cap), sources)
    moves = (from_slot[:, None] == lax.broadcasted_iota(jnp.int32, (slots, slots), 1)).astype(BF16)
    pre_own = jnp.dot(moves, saved_pre[0, 0], preferred_element_type=F32).astype(BF16)
    pre_own = pre_own.reshape(sources, cap, 2 * hidden)
    pre = jnp.stack([pre_own, swap_dp(pre_own)], axis=1).reshape(2, slots, 2 * hidden)

    weights = expert_weights[0]
    down_part = weights[:, 2 * hidden :]
    gate_up_part = weights[:, : 2 * hidden]

    def pack(blocks):
        kept, sent = [], []
        for h in range(nz):
            packed = jnp.einsum(
                "rpt,rtd->rpd", pick[h], blocks[h], preferred_element_type=F32
            ).astype(BF16).reshape(2, nx, 2, cap, half)
            for t in range(nx):
                rows = packed[:, t] if t == 0 else move_x(packed[:, t], t)
                kept.append(rows[:, 0])
                sent.append(rows[:, 1])
        return [
            jnp.stack(kept).reshape(slots, half),
            swap_core(jnp.stack(sent).reshape(slots, half)),
        ]

    def swap_replicas(v):
        flipped = v.reshape(near, 2, cap, v.shape[-1])[:, ::-1].reshape(v.shape)
        return swap_dp(flipped)

    grads = regroup(out_grad)
    acts = regroup(activations)
    grad_blocks = gather_z(grads)
    acts, grad_blocks[-1] = lax.optimization_barrier((acts, grad_blocks[-1]))
    act_blocks = gather_z(acts)
    grad_rows = pack(grad_blocks)

    gate_up, scaled, token_probs = [], [], []
    for i in range(2):
        part = jnp.dot(grad_rows[i], down_part, preferred_element_type=F32)
        down_grad = part + swap_replicas(part.astype(BF16)).astype(F32)
        gate = pre[i, :, :hidden].astype(F32)
        up = pre[i, :, hidden:].astype(F32)
        sig = jax.nn.sigmoid(gate)
        act = gate * sig
        hidden_act = act * up
        slot_prob = jnp.sum(hidden_act * down_grad, axis=1).astype(BF16).astype(F32)
        slot_prob = slot_prob.reshape(near, 2, cap)[:, 0, :, None]
        own = chosen_mine[i * near : (i + 1) * near, 0]
        token_probs.append(jnp.sum(jnp.where(own, slot_prob, 0.0), axis=1))
        dh = columns[i] * down_grad
        gate_up.append(
            jnp.concatenate(
                [dh * up * sig * (1.0 + gate * (1.0 - sig)), dh * act], axis=1
            ).astype(BF16)
        )
        scaled.append((columns[i] * hidden_act).astype(BF16))

    def row_grad(i):
        return lax.dot_general(
            gate_up[i], gate_up_part, (((1,), (1,)), ((), ())), preferred_element_type=F32
        ).astype(BF16)

    far_rows = swap_core(row_grad(1)).reshape(near, 2, cap, half)
    near_rows = row_grad(0).reshape(near, 2, cap, half)

    total = None
    for h in range(nz - 1, -1, -1):
        parts = []
        for t in range(nx):
            both = jnp.stack([near_rows[h * nx + t], far_rows[h * nx + t]], axis=1)
            parts.append(both if t == 0 else move_x(both, -t))
        spread = jnp.einsum(
            "rpt,rpd->rtd",
            pick[h],
            jnp.stack(parts, axis=1).reshape(2, 2 * nx * cap, half),
            preferred_element_type=F32,
        )
        total = spread if total is None else spread + move_z(total.astype(BF16), -1).astype(F32)
    total = total.astype(BF16)
    kept, back_half = total[0], swap_dp(total[1])
    input_grad = jnp.concatenate(
        [jnp.where(replica == 0, kept, back_half), jnp.where(replica == 0, back_half, kept)], axis=1
    )

    act_rows = pack(act_blocks)

    weight_grad = weight_outer(act_rows, grad_rows, gate_up, scaled)[None]

    source = jnp.arange(sources)
    s_ctx, s_z = source // nz, source % nz
    place_of = (
        jnp.bitwise_xor(s_ctx % 2, core_at) * near
        + (z_at - s_z) % nz * nx
        + (x_at - s_ctx // 2) % nx
    )
    outgoing = permuted(place_of, jnp.concatenate(token_probs).astype(BF16))
    back = lax.all_to_all(outgoing, PLANE, split_axis=0, concat_axis=0, tiled=True)
    experts = lax.broadcasted_iota(jnp.int32, (sources, tokens, top_k), 0)
    prob_grad = jnp.sum(
        jnp.where(routes[None] == experts, back[:, :, None].astype(F32), 0.0), axis=0
    ).astype(BF16)
    return (input_grad, prob_grad, weight_grad)


def solution(mesh):
    placed = (
        P(("ctx", "tp", "dp"), None),
        P(("ctx", "tp", "dp"), None),
        P(("ctx", "tp", "dp"), None),
        P(("ctx", "tp", "dp"), None),
        P(("ctx", "tp"), "dp", None, None),
        P(("ctx", "tp"), "dp", None),
    )
    return jax.shard_map(
        body,
        mesh=mesh,
        in_specs=placed,
        out_specs=(
            P(("ctx", "tp", "dp"), None),
            P(("ctx", "tp", "dp"), None),
            P(("ctx", "tp"), "dp", None),
        ),
        check_vma=False,
    )
```
